128 devices in a mesh: section: 8 (over z, y_lo), seq: 16 (over y_hi, x, core).
Axes of the slice: x: 4, y: 4 (y_hi: 2, y_lo: 2; y = y_hi * 2 + y_lo), z: 4, core: 2. Of those that a mesh axis runs over, the one named last changes fastest.
Arguments:
- qkv: bfloat16 [8, 1536, 3, 4096], P('section', 'seq'), may hold values from -5 to 5
- cache: bfloat16 [2, 24, 512, 4096], P(None, 'section', None, 'seq'), may hold values from -5 to 5
- window: int32 [8], P('section'), may hold values from 1 to 24, as said below
Outputs:
- attended: bfloat16 [8, 1536, 4096], P('section', 'seq')
- new_cache: bfloat16 [2, 24, 512, 4096], P(None, 'section', None, 'seq')
The draws below stay inside these ranges and needn't reach their ends.
Inputs may be any that keep to these rules, and one draw needn't show every extreme that they name: `window`: some section attends all 24 cache frames and some section only the newest.
All inputs are finite; a program needn't handle non-finite values.
Results may differ from the reference program's by a relative error of at most 0.02.
Values may be sent and summed in bfloat16 or wider, within the bound.
No kernel may reach another device: no remote copies, remote signals or barrier semaphores. Data moves between devices by JAX's collectives and lax.ppermute only.
A program may use at most 192 MiB of HBM per device.

```python
import math
import jax
import jax.numpy as jnp
from jax import lax

HEADS = 32
HD = 128
CF = 3
SPAN = 1536
FT = 512
CFR = 24
SECTIONS = 8
HH = 4096


def draw_qkv(key, part):
    key = jax.random.fold_in(key, 11)
    shape = (SECTIONS, SPAN, 3, HH)
    base = jnp.clip(jax.random.normal(key, shape, jnp.float32), -5.0, 5.0)
    return base.astype(jnp.bfloat16)


def draw_cache(key, part):
    key = jax.random.fold_in(key, 13)
    shape = (2, CFR, FT, HH)
    base = jnp.clip(jax.random.normal(key, shape, jnp.float32), -5.0, 5.0)
    return base.astype(jnp.bfloat16)


def draw_window(key, part):
    key = jax.random.fold_in(key, 5)
    counts = jax.random.randint(key, (SECTIONS,), 1, CFR + 1)
    order = jax.random.permutation(jax.random.fold_in(key, 6), SECTIONS)
    counts = counts.at[order[0]].set(CFR)
    counts = counts.at[order[1]].set(1)
    return counts.astype(jnp.int32)


def setup_inputs(seed: int = 0) -> dict:
    key_of = jax.random.split(jax.random.key(seed), 4)
    qkv = draw_qkv(jax.random.fold_in(key_of[3], 71), 0)
    cache = draw_cache(jax.random.fold_in(key_of[3], 71), 0)
    window = draw_window(jax.random.fold_in(key_of[3], 71), 0)
    return {"qkv": qkv, "cache": cache, "window": window}


def reference(qkv, cache, window):
    scale = 1.0 / math.sqrt(HD)
    cache_keys = cache[0].reshape(CFR * FT, HEADS, HD)
    cache_values = cache[1].reshape(CFR * FT, HEADS, HD)
    key_frame = jnp.concatenate([jnp.arange(CFR * FT) // FT, jnp.arange(SPAN) // FT]).astype(jnp.int32)
    in_cache = jnp.concatenate([jnp.ones((CFR * FT,), bool), jnp.zeros((SPAN,), bool)])
    query_frame = (jnp.arange(SPAN) // FT).astype(jnp.int32)

    def one_denoiser(item):
        block, limit = item
        parts = block.reshape(SPAN, 3, HEADS, HD)
        keys_all = jnp.concatenate([cache_keys, parts[:, 1]], 0)
        values_all = jnp.concatenate([cache_values, parts[:, 2]], 0)
        allowed = jnp.where(in_cache[None, :], key_frame[None, :] >= CFR - limit, key_frame[None, :] <= query_frame[:, None])

        def one_head(triple):
            query, keys, values = triple
            scores = jnp.dot(query, keys.T, preferred_element_type=jnp.float32) * scale
            top = lax.optimization_barrier(jnp.max(jnp.where(allowed, scores, -jnp.inf), axis=-1))
            weights = jnp.where(allowed, jnp.exp(scores - top[:, None]), 0.0)
            total = lax.optimization_barrier(jnp.sum(weights, axis=-1))
            mixed = jnp.dot(weights.astype(jnp.bfloat16), values, preferred_element_type=jnp.float32)
            return (mixed / total[:, None]).astype(jnp.bfloat16)
        heads_out = lax.map(one_head, (jnp.moveaxis(parts[:, 0], 1, 0), jnp.moveaxis(keys_all, 1, 0), jnp.moveaxis(values_all, 1, 0)))
        return jnp.moveaxis(heads_out, 0, 1).reshape(SPAN, HH)
    attended = lax.map(one_denoiser, (qkv, window))
    fresh = jnp.moveaxis(qkv[SECTIONS - 1, :, 1:3], 1, 0).reshape(2, CF, FT, HH)
    new_cache = jnp.concatenate([cache[:, CF:], fresh], 1)
    return (attended, new_cache)
```

```python
import functools
import math

import jax
import jax.numpy as jnp
from jax import lax
from jax.experimental import pallas as pl
from jax.experimental.pallas import tpu as pltpu
from jax.sharding import Mesh, PartitionSpec as P

HD = 128
CF = 3
FT = 512
SPAN = 1536
CFR = 24
SCALE = math.log2(math.e) / math.sqrt(HD)
TRUST = 2.0**100
VMEM_LIMIT = 56 << 20


def score(query, keys):
    return lax.dot_general(query, keys, (((1,), (1,)), ((), ())), preferred_element_type=jnp.float32)


def lanes(column, count):
    return jnp.concatenate([column] * (count // HD), -1)


def with_ones(values):
    return jnp.concatenate([values, jnp.ones(values.shape, values.dtype)], -1)


def mix(weights, values):
    return jnp.dot(weights.astype(jnp.bfloat16), with_ones(values), preferred_element_type=jnp.float32)


def piece_loop(info_ref, base_at, count, pieces, waits, read_q, acc_ref, top_ref, start_ref):
    def first_frame(section, piece):
        return jnp.clip(CFR - info_ref[section] - info_ref[base_at + piece], 0, CF)

    def one(index, carry):
        piece, section = index // 2, index % 2

        @pl.when(section == 0)
        def _():
            waits(piece)

        first = first_frame(section, piece)

        def add(start, size):
            rows = pl.ds(start, size)
            weights = jnp.exp2(
                score(read_q(section), pieces[piece, 0, rows, :]) * SCALE - lanes(top_ref[section], size)
            )
            acc_ref[section] += mix(weights, pieces[piece, 1, rows, :])

        @pl.when(first == 0)
        def _():
            add(0, CF * FT)

        @pl.when(first > 0)
        def _():
            def frame(f, inner):
                add(pl.multiple_of(f * FT, FT), FT)
                return inner

            lax.fori_loop(first, CF, frame, 0)

        return carry

    lax.fori_loop(0, 2 * count, one, 0)

    def check(section, carry):
        safe = jnp.max(acc_ref[section, :, HD:]) < TRUST

        @pl.when(jnp.logical_not(safe))
        def _():
            acc_ref[section] = start_ref[section]

            def again(index, inner):
                piece, part = index // CF, index % CF
                tile = pl.ds(pl.multiple_of(part * FT, FT), FT)

                def frame(f, deep):
                    rows = pl.ds(pl.multiple_of(f * FT, FT), FT)
                    scores = score(read_q(section, tile), pieces[piece, 0, rows, :]) * SCALE
                    before = top_ref[section, tile, :]
                    top = jnp.maximum(before, jnp.max(scores, axis=-1, keepdims=True))
                    weights = jnp.exp2(scores - lanes(top, FT))
                    acc_ref[section, tile, :] = acc_ref[section, tile, :] * lanes(
                        jnp.exp2(before - top), 2 * HD
                    ) + mix(weights, pieces[piece, 1, rows, :])
                    top_ref[section, tile, :] = top
                    return deep

                lax.fori_loop(first_frame(section, piece), CF, frame, 0)
                return inner

            lax.fori_loop(0, CF * count, again, 0)

        return carry

    lax.fori_loop(0, 2, check, 0)


def first_kernel(
    base_at, count, info_ref, spread_ref, *refs
):
    sources, refs = refs[:count], refs[count:]
    query_ref, acc_ref, top_ref, fresh_ref, pieces, keys, values, start, sems = refs
    copies = [pltpu.make_async_copy(sources[i], pieces.at[i], sems.at[i]) for i in range(count)]
    for copy in copies:
        copy.start()

    def own(section, carry):
        for j in range(16):
            rows = pl.ds(j * 96, 96)
            query_ref[section, rows, :] = spread_ref[section, j, 0]
            keys[rows, :] = spread_ref[section, j, 1]
            values[rows, :] = spread_ref[section, j, 2]
        for i in range(CF):
            tile = pl.ds(i * FT, FT)
            size = (i + 1) * FT
            scores = score(query_ref[section, tile, :], keys[:size, :]) * SCALE
            top = jnp.broadcast_to(jnp.max(scores, axis=-1, keepdims=True), (FT, HD))
            top_ref[section, tile, :] = top
            acc_ref[section, tile, :] = mix(jnp.exp2(scores - lanes(top, size)), values[:size, :])
        return carry

    lax.fori_loop(0, 2, own, 0)
    fresh_ref[0] = keys[...]
    fresh_ref[1] = values[...]
    start[...] = acc_ref[...]

    def waits(piece):
        for i in range(count):
            @pl.when(piece == i)
            def _():
                copies[i].wait()

    def read_q(section, rows=slice(None)):
        return query_ref[section, rows, :]

    piece_loop(info_ref, base_at, count, pieces, waits, read_q, acc_ref, top_ref, start)


def later_kernel(base_at, layout, last, info_ref, query_ref, start_ref, top_in_ref, *refs):
    total = sum(len(parts) for parts in layout)
    count = len(layout)
    sources, refs = refs[:total], refs[total:]
    if last:
        out_ref, pieces, acc_ref, top_ref, sems = refs
    else:
        acc_ref, top_ref, pieces, sems = refs
    copies, at = [], 0
    for i, parts in enumerate(layout):
        group = []
        for part in parts:
            target = pieces.at[i] if part is None else pieces.at[i, part]
            group.append(pltpu.make_async_copy(sources[at], target, sems.at[at]))
            at += 1
        copies.append(group)
    for group in copies:
        for copy in group:
            copy.start()
    acc_ref[...] = start_ref[...]
    top_ref[...] = top_in_ref[...]

    def waits(piece):
        for i in range(count):
            @pl.when(piece == i)
            def _():
                for copy in copies[i]:
                    copy.wait()

    def read_q(section, rows=slice(None)):
        return query_ref[section, rows, :]

    piece_loop(info_ref, base_at, count, pieces, waits, read_q, acc_ref, top_ref, start_ref)
    if last:
        def finish(section, carry):
            out_ref[section] = (acc_ref[section, :, :HD] / acc_ref[section, :, HD:]).astype(jnp.bfloat16)
            return carry

        lax.fori_loop(0, 2, finish, 0)


def cost(frames):
    pairs = 2 * SPAN * frames * FT
    return pl.CostEstimate(flops=8 * pairs * HD, bytes_accessed=8 << 20, transcendentals=pairs)


SMEM = pl.BlockSpec(memory_space=pltpu.SMEM)
VMEM = pl.BlockSpec(memory_space=pltpu.VMEM)
ANY = pl.BlockSpec(memory_space=pl.ANY)
STATE = (
    jax.ShapeDtypeStruct((2, SPAN, 2 * HD), jnp.float32),
    jax.ShapeDtypeStruct((2, SPAN, HD), jnp.float32),
)


def attend_first(info, spread, sources, base_at):
    count = len(sources)
    return pl.pallas_call(
        functools.partial(first_kernel, base_at, count),
        out_shape=(
            jax.ShapeDtypeStruct((2, SPAN, HD), jnp.bfloat16),
            *STATE,
            jax.ShapeDtypeStruct((2, SPAN, HD), jnp.bfloat16),
        ),
        in_specs=[SMEM, VMEM] + [ANY] * count,
        out_specs=(VMEM,) * 4,
        scratch_shapes=[
            pltpu.VMEM((count, 2, SPAN, HD), jnp.bfloat16),
            pltpu.VMEM((SPAN, HD), jnp.bfloat16),
            pltpu.VMEM((SPAN, HD), jnp.bfloat16),
            pltpu.VMEM((2, SPAN, 2 * HD), jnp.float32),
            pltpu.SemaphoreType.DMA((count,)),
        ],
        compiler_params=pltpu.CompilerParams(vmem_limit_bytes=VMEM_LIMIT),
        cost_estimate=cost(2 + 2 * count),
        name="attend_first",
    )(info, spread, *sources)


def attend_later(info, query, acc, top, groups, base_at, last):
    layout = [(None,) if len(group) == 1 else (0, 1) for group in groups]
    sources = [array for group in groups for array in group]
    count = len(groups)
    pieces = pltpu.VMEM((count, 2, SPAN, HD), jnp.bfloat16)
    sems = pltpu.SemaphoreType.DMA((len(sources),))
    if last:
        out_shape = jax.ShapeDtypeStruct((2, SPAN, HD), jnp.bfloat16)
        out_specs = VMEM
        scratch = [
            pieces,
            pltpu.VMEM((2, SPAN, 2 * HD), jnp.float32),
            pltpu.VMEM((2, SPAN, HD), jnp.float32),
            sems,
        ]
    else:
        out_shape, out_specs, scratch = STATE, (VMEM, VMEM), [pieces, sems]
    return pl.pallas_call(
        functools.partial(later_kernel, base_at, layout, last),
        out_shape=out_shape,
        in_specs=[SMEM, VMEM, VMEM, VMEM] + [ANY] * len(sources),
        out_specs=out_specs,
        scratch_shapes=scratch,
        compiler_params=pltpu.CompilerParams(vmem_limit_bytes=VMEM_LIMIT),
        cost_estimate=cost(2 * count),
        name="attend_last" if last else "attend_next",
    )(info, query, acc, top, *sources)


def turn(value, axis, steps):
    count = lax.axis_size(axis)
    return lax.ppermute(value, axis, [(i, (i + steps) % count) for i in range(count)])


def per_device(qkv, cache, window):
    z, yl = lax.axis_index("z"), lax.axis_index("yl")
    planes = lax.axis_size("z")
    rows = qkv.shape[1]
    heads = qkv.shape[3] // HD
    near = cache.shape[1]

    def half(which):
        return lax.dynamic_slice_in_dim(cache, which * HD, HD, 3).reshape(2, near * FT, HD)

    mine, other = half(yl), half(1 - yl)
    mine_up, mine_down = turn(mine, "z", 1), turn(mine, "z", -1)
    swap = turn(other, "yl", 1)
    swap_up, swap_down = turn(swap, "z", 1), turn(swap, "z", -1)
    mine_keys, mine_values = turn(mine_up[0], "z", 1), turn(mine_down[1], "z", -1)
    swap_keys, swap_values = turn(swap_up[0], "z", 1), turn(swap_down[1], "z", -1)

    window_other = turn(window, "yl", 1)
    windows = jnp.where(yl == 0, jnp.concatenate([window, window_other]), jnp.concatenate([window_other, window]))
    plane = jnp.array([0, 0, -1, -1, 1, 1, 2, 2], jnp.int32)
    side = jnp.where(jnp.array([0, 1] * 4) == 0, yl, 1 - yl)
    bases = near * (2 * ((z + plane) % planes) + side)
    info = jnp.concatenate([windows, bases]).astype(jnp.int32)

    tokens = jnp.swapaxes(qkv[0], 0, 1).reshape(3, rows, heads // 2, 2, HD)
    tokens = tokens.transpose(3, 2, 0, 1, 4).reshape(heads, 3 * rows, HD)
    spread = lax.all_to_all(tokens, ("yl", "seq"), 0, 0, tiled=True)
    spread = spread.reshape(2, heads // 2, 3, rows, HD)

    query, acc, top, fresh = attend_first(info, spread, [mine, swap], 2)
    acc, top = attend_later(
        info, query, acc, top, [[mine_up], [swap_up], [mine_down], [swap_down]], 4, False
    )
    result = attend_later(
        info, query, acc, top, [[mine_keys, mine_values], [swap_keys, swap_values]], 8, True
    )
    returned = lax.all_to_all(result.reshape(heads, rows, HD), ("yl", "seq"), 0, 0, tiled=True)
    attended = returned.reshape(2, heads // 2, rows, HD).transpose(2, 1, 0, 3).reshape(1, rows, heads * HD)

    final = z == planes - 1
    sent = jnp.where(yl == 1, mine, jnp.where(final, fresh, mine_down))
    kept = jnp.where(yl == 0, swap, jnp.where(final, fresh, swap_down))
    got = turn(sent, "yl", 1)
    new_cache = jnp.where(yl == 0, jnp.concatenate([kept, got], -1), jnp.concatenate([got, kept], -1))
    return attended, new_cache.reshape(cache.shape)


def solution(mesh):
    parts = Mesh(mesh.devices.reshape(4, 2, 16), ("z", "yl", "seq"))
    section = ("z", "yl")
    in_specs = (P(section, "seq", None, None), P(None, section, None, "seq"), P(section))
    out_specs = (P(section, "seq", None), P(None, section, None, "seq"))
    return jax.shard_map(
        per_device, mesh=parts, in_specs=in_specs, out_specs=out_specs, check_vma=False
    )
```

```python
import functools
import math

import jax
import jax.numpy as jnp
from jax import lax
from jax.experimental import pallas as pl
from jax.experimental.pallas import tpu as pltpu
from jax.sharding import Mesh, PartitionSpec as P

HD = 128
CF = 3
FT = 512
SPAN = 1536
CFR = 24
BASES = 2
NOTE = 16
SCALE = math.log2(math.e) / math.sqrt(HD)
TRUST = 2.0**100
VMEM_LIMIT = 52 << 20


def score(query, keys):
    scores = lax.dot_general(keys, query, (((1,), (1,)), ((), ())), preferred_element_type=jnp.float32)
    return scores * SCALE


def mix(weights, values):
    return lax.dot_general(
        values, weights.astype(jnp.bfloat16), (((0,), (0,)), ((), ())), preferred_element_type=jnp.float32
    )


def fold(weights):
    return jnp.sum(weights.reshape(weights.shape[0] // 8, 8, weights.shape[1]), axis=0)


def highest(scores):
    return jnp.broadcast_to(jnp.max(scores, axis=0, keepdims=True), (8, scores.shape[1]))


def tile_of(part):
    return pl.ds(pl.multiple_of(part * FT, FT), FT)


def attend_kernel(first_piece, layout, with_own, last, *refs):
    refs = list(refs)
    info_ref, query_ref = refs.pop(0), refs.pop(0)
    if first_piece:
        acc_in_ref, total_in_ref, top_in_ref = refs.pop(0), refs.pop(0), refs.pop(0)
    if with_own:
        spread_ref = refs.pop(0)
    sources = [refs.pop(0) for parts in layout for _ in parts]
    if last:
        out_ref = refs.pop(0)
    else:
        acc_ref, total_ref, top_ref = refs.pop(0), refs.pop(0), refs.pop(0)
    pieces, sems = refs.pop(0), refs.pop(0)
    if last:
        acc_ref, total_ref, top_ref = refs.pop(0), refs.pop(0), refs.pop(0)
    if with_own:
        own = refs.pop(0)

    count = len(layout)
    copies, at = [], 0
    for i, parts in enumerate(layout):
        copies.append([])
        for part in parts:
            target = pieces.at[i] if part is None else pieces.at[i, part]
            source = sources[at].at[..., pl.ds(0, SPAN), :]
            copies[-1].append(pltpu.make_async_copy(source, target, sems.at[at]))
            copies[-1][-1].start()
            at += 1

    def first_frame(section, piece):
        return jnp.clip(CFR - info_ref[section] - info_ref[BASES + first_piece + piece], 0, CF)

    def blank(section, piece):
        newest = lax.fori_loop(
            0, first_piece + piece, lambda i, most: jnp.maximum(most, info_ref[BASES + i]), jnp.int32(-CFR)
        )
        return newest + CF <= CFR - info_ref[section]

    def begin(section):
        if first_piece:
            acc_ref[section] = acc_in_ref[section]
            total_ref[section] = total_in_ref[section]
            top_ref[section] = top_in_ref[section]
        else:
            acc_ref[section] = jnp.zeros(acc_ref.shape[1:], acc_ref.dtype)
            total_ref[section] = jnp.zeros(total_ref.shape[1:], total_ref.dtype)
            top_ref[section] = jnp.zeros(top_ref.shape[1:], top_ref.dtype)

    begin(0)
    begin(1)

    def add(section, tile, keys, values):
        weights = jnp.exp2(score(query_ref[section, tile, :], keys) - top_ref[section, :1, tile])
        total_ref[section, :, tile] += fold(weights)
        acc_ref[section, :, tile] += mix(weights, values)

    if with_own:
        def add_own(section, carry):
            for j in range(spread_ref.shape[1]):
                rows = pl.ds(j * spread_ref.shape[3], spread_ref.shape[3])
                own[section, 0, rows, :] = spread_ref[section, j, 0]
                own[section, 1, rows, :] = spread_ref[section, j, 1]

            @pl.when(blank(section, 0))
            def _():
                for i in range(CF):
                    tile = pl.ds(i * FT, FT)
                    top_ref[section, :, tile] = highest(score(query_ref[section, tile, :], own[section, 0, tile, :]))

            for i in range(CF):
                keys = pl.ds(0, (i + 1) * FT)
                add(section, pl.ds(i * FT, FT), own[section, 0, keys, :], own[section, 1, keys, :])
            return carry

        lax.fori_loop(0, 2, add_own, 0)

    def one(index, carry):
        piece, section = index // 2, index % 2
        for i in range(count):
            @pl.when(index == 2 * i)
            def _():
                for copy in copies[i]:
                    copy.wait()

        first = first_frame(section, piece)
        everyone = pl.ds(0, SPAN)
        if not with_own:
            @pl.when(jnp.logical_and(first < CF, blank(section, piece)))
            def _():
                top_ref[section] = highest(score(query_ref[section], pieces[piece, 0, tile_of(first), :]))

        @pl.when(first == 0)
        def _():
            add(section, everyone, pieces[piece, 0], pieces[piece, 1])

        @pl.when(first > 0)
        def _():
            def frame(f, inner):
                add(section, everyone, pieces[piece, 0, tile_of(f), :], pieces[piece, 1, tile_of(f), :])
                return inner

            lax.fori_loop(first, CF, frame, 0)

        return carry

    lax.fori_loop(0, 2 * count, one, 0)

    def check(section, carry):
        safe = jnp.max(total_ref[section]) < TRUST

        @pl.when(jnp.logical_not(safe))
        def _():
            begin(section)

            @pl.when(blank(section, 0))
            def _():
                top_ref[section] = jnp.full(top_ref.shape[1:], -1e30, top_ref.dtype)

            def update(tile, keys, values):
                scores = score(query_ref[section, tile, :], keys)
                before = top_ref[section, :, tile]
                top = jnp.maximum(before, highest(scores))
                factor = jnp.exp2(before - top)
                weights = jnp.exp2(scores - top[:1])
                total_ref[section, :, tile] = total_ref[section, :, tile] * factor + fold(weights)
                acc_ref[section, :, tile] = acc_ref[section, :, tile] * factor[:1] + mix(weights, values)
                top_ref[section, :, tile] = top

            def again(part, inner):
                tile = tile_of(part)
                if with_own:
                    def own_frame(f, deep):
                        update(tile, own[section, 0, tile_of(f), :], own[section, 1, tile_of(f), :])
                        return deep

                    lax.fori_loop(0, part + 1, own_frame, 0)

                def one_piece(piece, deep):
                    def frame(f, deeper):
                        update(tile, pieces[piece, 0, tile_of(f), :], pieces[piece, 1, tile_of(f), :])
                        return deeper

                    lax.fori_loop(first_frame(section, piece), CF, frame, 0)
                    return deep

                lax.fori_loop(0, count, one_piece, 0)
                return inner

            lax.fori_loop(0, CF, again, 0)

        return carry

    lax.fori_loop(0, 2, check, 0)
    if last:
        def finish(section, carry):
            total = jnp.sum(total_ref[section], axis=0, keepdims=True)
            out_ref[section] = (acc_ref[section] / total).T.astype(jnp.bfloat16)
            return carry

        lax.fori_loop(0, 2, finish, 0)


SMEM = pl.BlockSpec(memory_space=pltpu.SMEM)
VMEM = pl.BlockSpec(memory_space=pltpu.VMEM)
ANY = pl.BlockSpec(memory_space=pl.ANY)
KV = ((2, SPAN, HD), jnp.bfloat16)
STATE = (((2, HD, SPAN), jnp.float32), ((2, 8, SPAN), jnp.float32), ((2, 8, SPAN), jnp.float32))


def attend(info, query, state, spread, groups, first_piece, last, name):
    layout = [(None,) if len(group) == 1 else (0, 1) for group in groups]
    sources = [array for group in groups for array in group]
    count, with_own = len(groups), spread is not None
    outs = [jax.ShapeDtypeStruct(*kind) for kind in ([KV] if last else STATE)]
    scratch = [pltpu.VMEM((count, 2, SPAN, HD), jnp.bfloat16), pltpu.SemaphoreType.DMA((len(sources),))]
    if last:
        scratch += [pltpu.VMEM(*kind) for kind in STATE]
    if with_own:
        scratch.append(pltpu.VMEM((2, 2, SPAN, HD), jnp.bfloat16))
    dense = [query, *state] + ([spread] if with_own else [])
    pairs = 2 * SPAN * FT * (CF * count + 2 * with_own) * 3 // 4
    return pl.pallas_call(
        functools.partial(attend_kernel, first_piece, layout, with_own, last),
        out_shape=outs,
        in_specs=[SMEM] + [VMEM] * len(dense) + [ANY] * len(sources),
        out_specs=[VMEM] * len(outs),
        scratch_shapes=scratch,
        compiler_params=pltpu.CompilerParams(vmem_limit_bytes=VMEM_LIMIT),
        cost_estimate=pl.CostEstimate(flops=8 * pairs * HD, bytes_accessed=8 << 20, transcendentals=pairs),
        name=name,
    )(info, *dense, *sources)


def prepare_kernel(window_ref, tokens_ref, cache_ref, query_ref, own_ref, mine_ref, other_ref):
    for j in range(query_ref.shape[1]):
        for side in range(2):
            columns = pl.ds((2 * j + side) * HD, HD)
            query_ref[side, j] = tokens_ref[0, :, columns]
            own_ref[side, j, 0] = tokens_ref[1, :, columns]
            own_ref[side, j, 1] = tokens_ref[2, :, columns]
    odd = lax.axis_index("yl") == 1
    low, high = cache_ref[..., :HD], cache_ref[..., HD:]
    mine_ref[...] = jnp.where(odd, high, low)
    other_ref[:, pl.ds(0, cache_ref.shape[1]), :] = jnp.where(odd, low, high)
    note = other_ref.at[:, pl.ds(cache_ref.shape[1], NOTE), :]
    note[...] = jnp.full(note.shape, window_ref[0], jnp.int32).astype(other_ref.dtype)


def prepare(window, tokens, cache, steps=2):
    parts, rows, width = tokens.shape
    pairs = width // (2 * HD)
    step = pairs // steps
    kinds, length, both = cache.shape
    return pl.pallas_call(
        prepare_kernel,
        grid=(steps,),
        out_shape=(
            jax.ShapeDtypeStruct((2, pairs, rows, HD), tokens.dtype),
            jax.ShapeDtypeStruct((2, pairs, 2, rows, HD), tokens.dtype),
            jax.ShapeDtypeStruct((kinds, length, both // 2), cache.dtype),
            jax.ShapeDtypeStruct((kinds, length + NOTE, both // 2), cache.dtype),
        ),
        in_specs=[
            SMEM,
            pl.BlockSpec((parts, rows, 2 * step * HD), lambda i: (0, 0, i)),
            pl.BlockSpec((kinds // steps, length, both), lambda i: (i, 0, 0)),
        ],
        out_specs=(
            pl.BlockSpec((2, step, rows, HD), lambda i: (0, i, 0, 0)),
            pl.BlockSpec((2, step, 2, rows, HD), lambda i: (0, i, 0, 0, 0)),
            pl.BlockSpec((kinds // steps, length, both // 2), lambda i: (i, 0, 0)),
            pl.BlockSpec((kinds // steps, length + NOTE, both // 2), lambda i: (i, 0, 0)),
        ),
        compiler_params=pltpu.CompilerParams(vmem_limit_bytes=VMEM_LIMIT),
        name="prepare",
    )(window, tokens, cache)


def by_token_kernel(heads_ref, out_ref):
    sides, pairs, _, _ = heads_ref.shape
    for side in range(sides):
        for j in range(pairs):
            out_ref[:, pl.ds((sides * j + side) * HD, HD)] = heads_ref[side, j]


def by_token(heads):
    sides, pairs, rows, _ = heads.shape
    return pl.pallas_call(
        by_token_kernel,
        out_shape=jax.ShapeDtypeStruct((rows, sides * pairs * HD), heads.dtype),
        in_specs=[VMEM],
        out_specs=VMEM,
        name="by_token",
    )(heads)


def turn(value, axis, steps):
    count = lax.axis_size(axis)
    return lax.ppermute(value, axis, [(i, (i + steps) % count) for i in range(count)])


def per_device(qkv, cache, window):
    z, yl = lax.axis_index("z"), lax.axis_index("yl")
    planes = lax.axis_size("z")
    rows = qkv.shape[1]
    heads = qkv.shape[3] // HD
    near = cache.shape[1]

    query, own, mine, other = prepare(window, jnp.swapaxes(qkv[0], 0, 1), cache.reshape(2, near * FT, 2 * HD))
    query = lax.all_to_all(query.reshape(heads, rows, HD), ("yl", "seq"), 0, 0, tiled=True).reshape(2, SPAN, HD)
    own = lax.all_to_all(own.reshape(heads, 2 * rows, HD), ("yl", "seq"), 0, 0, tiled=True)
    own = own.reshape(2, heads // 2, 2, rows, HD)
    swap = turn(other, "yl", 1)
    mine_up, mine_down = turn(mine, "z", 1), turn(mine, "z", -1)
    swap_up, swap_down = turn(swap, "z", 1), turn(swap, "z", -1)
    mine_far = [turn(mine_up[0], "z", 1), turn(mine_down[1], "z", -1)]
    swap_far = turn(swap, "z", 2)

    window_other = swap[0, near * FT, :1].astype(jnp.int32)
    windows = jnp.where(yl == 0, jnp.concatenate([window, window_other]), jnp.concatenate([window_other, window]))
    plane = jnp.array([0, -1, 1, 0, 2, -1, 1, 2], jnp.int32)
    side = jnp.where(jnp.array([0, 0, 0, 1, 0, 1, 1, 1]) == 0, yl, 1 - yl)
    bases = near * (2 * ((z + plane) % planes) + side)
    info = jnp.concatenate([windows, bases]).astype(jnp.int32)

    state = attend(info, query, (), None, [[mine], [mine_up], [mine_down], [swap], mine_far], 0, False, "attend_early")
    (result,) = attend(info, query, state, own, [[swap_up], [swap_down], [swap_far]], 5, True, "attend_late")
    returned = lax.all_to_all(result.reshape(heads, rows, HD), ("yl", "seq"), 0, 0, tiled=True)
    attended = by_token(returned.reshape(2, heads // 2, rows, HD))[None]

    final = z == planes - 1
    fresh = own[1].transpose(1, 0, 2, 3).reshape(2, SPAN, HD)
    swap, swap_down = swap[:, :SPAN], swap_down[:, :SPAN]
    sent = jnp.where(yl == 1, mine, jnp.where(final, fresh, mine_down))
    kept = jnp.where(yl == 0, swap, jnp.where(final, fresh, swap_down))
    got = turn(sent, "yl", 1)
    new_cache = jnp.where(yl == 0, jnp.concatenate([kept, got], -1), jnp.concatenate([got, kept], -1))
    return attended, new_cache.reshape(cache.shape)


def solution(mesh):
    parts = Mesh(mesh.devices.reshape(4, 2, 16), ("z", "yl", "seq"))
    section = ("z", "yl")
    in_specs = (P(section, "seq", None, None), P(None, section, None, "seq"), P(section))
    out_specs = (P(section, "seq", None), P(None, section, None, "seq"))
    return jax.shard_map(
        per_device, mesh=parts, in_specs=in_specs, out_specs=out_specs, check_vma=False
    )
```

```python
import functools
import math

import jax
import jax.numpy as jnp
from jax import lax
from jax.experimental import pallas as pl
from jax.experimental.pallas import tpu as pltpu
from jax.sharding import Mesh, PartitionSpec as P

HD = 128
CF = 3
FT = 512
SPAN = 1536
CFR = 24
BASES = 2
NOTE = 16
SCALE = math.log2(math.e) / math.sqrt(HD)
TRUST = 2.0**100
VMEM_LIMIT = 52 << 20


def score(query, keys):
    scores = lax.dot_general(keys, query, (((1,), (1,)), ((), ())), preferred_element_type=jnp.float32)
    return scores * SCALE


def mix(weights, values):
    return lax.dot_general(
        values, weights.astype(jnp.bfloat16), (((0,), (0,)), ((), ())), preferred_element_type=jnp.float32
    )


def fold(weights):
    return jnp.sum(weights.reshape(weights.shape[0] // 8, 8, weights.shape[1]), axis=0)


def highest(scores):
    return jnp.broadcast_to(jnp.max(scores, axis=0, keepdims=True), (8, scores.shape[1]))


def tile_of(part):
    return pl.ds(pl.multiple_of(part * FT, FT), FT)


def attend_kernel(first_piece, layout, with_own, last, *refs):
    refs = list(refs)
    info_ref, query_ref = refs.pop(0), refs.pop(0)
    if first_piece:
        acc_in_ref, total_in_ref, top_in_ref = refs.pop(0), refs.pop(0), refs.pop(0)
    if with_own:
        spread_ref = refs.pop(0)
    sources = [refs.pop(0) for parts in layout for _ in parts]
    if last:
        out_ref = refs.pop(0)
    else:
        acc_ref, total_ref, top_ref = refs.pop(0), refs.pop(0), refs.pop(0)
    pieces, sems = refs.pop(0), refs.pop(0)
    if last:
        acc_ref, total_ref, top_ref = refs.pop(0), refs.pop(0), refs.pop(0)
    if with_own:
        own = refs.pop(0)

    count = len(layout)
    copies, at = [], 0
    for i, parts in enumerate(layout):
        copies.append([])
        for part in parts:
            target = pieces.at[i] if part is None else pieces.at[i, part]
            source = sources[at].at[..., pl.ds(0, SPAN), :]
            copies[-1].append(pltpu.make_async_copy(source, target, sems.at[at]))
            copies[-1][-1].start()
            at += 1

    def first_frame(section, piece):
        return jnp.clip(CFR - info_ref[section] - info_ref[BASES + first_piece + piece], 0, CF)

    def blank(section, piece):
        newest = lax.fori_loop(
            0, first_piece + piece, lambda i, most: jnp.maximum(most, info_ref[BASES + i]), jnp.int32(-CFR)
        )
        return newest + CF <= CFR - info_ref[section]

    def begin(section):
        if first_piece:
            acc_ref[section] = acc_in_ref[section]
            total_ref[section] = total_in_ref[section]
            top_ref[section] = top_in_ref[section]
        else:
            acc_ref[section] = jnp.zeros(acc_ref.shape[1:], acc_ref.dtype)
            total_ref[section] = jnp.zeros(total_ref.shape[1:], total_ref.dtype)
            top_ref[section] = jnp.zeros(top_ref.shape[1:], top_ref.dtype)

    begin(0)
    begin(1)

    def add(section, tile, keys, values):
        weights = jnp.exp2(score(query_ref[section, tile, :], keys) - top_ref[section, :1, tile])
        total_ref[section, :, tile] += fold(weights)
        acc_ref[section, :, tile] += mix(weights, values)

    if with_own:
        def add_own(section, carry):
            for j in range(spread_ref.shape[1]):
                rows = pl.ds(j * spread_ref.shape[3], spread_ref.shape[3])
                own[section, 0, rows, :] = spread_ref[section, j, 0]
                own[section, 1, rows, :] = spread_ref[section, j, 1]

            @pl.when(blank(section, 0))
            def _():
                for i in range(CF):
                    tile = pl.ds(i * FT, FT)
                    top_ref[section, :, tile] = highest(score(query_ref[section, tile, :], own[section, 0, tile, :]))

            for i in range(CF):
                keys = pl.ds(0, (i + 1) * FT)
                add(section, pl.ds(i * FT, FT), own[section, 0, keys, :], own[section, 1, keys, :])
            return carry

        lax.fori_loop(0, 2, add_own, 0)

    def one(index, carry):
        piece, section = index // 2, index % 2
        for i in range(count):
            @pl.when(index == 2 * i)
            def _():
                for copy in copies[i]:
                    copy.wait()

        first = first_frame(section, piece)
        everyone = pl.ds(0, SPAN)
        if not with_own:
            @pl.when(jnp.logical_and(first < CF, blank(section, piece)))
            def _():
                top_ref[section] = highest(score(query_ref[section], pieces[piece, 0, tile_of(first), :]))

        @pl.when(first == 0)
        def _():
            add(section, everyone, pieces[piece, 0], pieces[piece, 1])

        @pl.when(first > 0)
        def _():
            def frame(f, inner):
                add(section, everyone, pieces[piece, 0, tile_of(f), :], pieces[piece, 1, tile_of(f), :])
                return inner

            lax.fori_loop(first, CF, frame, 0)

        return carry

    lax.fori_loop(0, 2 * count, one, 0)

    def check(section, carry):
        safe = jnp.max(total_ref[section]) < TRUST

        @pl.when(jnp.logical_not(safe))
        def _():
            begin(section)

            @pl.when(blank(section, 0))
            def _():
                top_ref[section] = jnp.full(top_ref.shape[1:], -1e30, top_ref.dtype)

            def update(tile, keys, values):
                scores = score(query_ref[section, tile, :], keys)
                before = top_ref[section, :, tile]
                top = jnp.maximum(before, highest(scores))
                factor = jnp.exp2(before - top)
                weights = jnp.exp2(scores - top[:1])
                total_ref[section, :, tile] = total_ref[section, :, tile] * factor + fold(weights)
                acc_ref[section, :, tile] = acc_ref[section, :, tile] * factor[:1] + mix(weights, values)
                top_ref[section, :, tile] = top

            def again(part, inner):
                tile = tile_of(part)
                if with_own:
                    def own_frame(f, deep):
                        update(tile, own[section, 0, tile_of(f), :], own[section, 1, tile_of(f), :])
                        return deep

                    lax.fori_loop(0, part + 1, own_frame, 0)

                def one_piece(piece, deep):
                    def frame(f, deeper):
                        update(tile, pieces[piece, 0, tile_of(f), :], pieces[piece, 1, tile_of(f), :])
                        return deeper

                    lax.fori_loop(first_frame(section, piece), CF, frame, 0)
                    return deep

                lax.fori_loop(0, count, one_piece, 0)
                return inner

            lax.fori_loop(0, CF, again, 0)

        return carry

    lax.fori_loop(0, 2, check, 0)
    if last:
        def finish(section, carry):
            total = jnp.sum(total_ref[section], axis=0, keepdims=True)
            out_ref[section] = (acc_ref[section] / total).T.astype(jnp.bfloat16)
            return carry

        lax.fori_loop(0, 2, finish, 0)


SMEM = pl.BlockSpec(memory_space=pltpu.SMEM)
VMEM = pl.BlockSpec(memory_space=pltpu.VMEM)
ANY = pl.BlockSpec(memory_space=pl.ANY)
KV = ((2, SPAN, HD), jnp.bfloat16)
STATE = (((2, HD, SPAN), jnp.float32), ((2, 8, SPAN), jnp.float32), ((2, 8, SPAN), jnp.float32))


def attend(info, query, state, spread, groups, first_piece, last, name):
    layout = [(None,) if len(group) == 1 else (0, 1) for group in groups]
    sources = [array for group in groups for array in group]
    count, with_own = len(groups), spread is not None
    outs = [jax.ShapeDtypeStruct(*kind) for kind in ([KV] if last else STATE)]
    scratch = [pltpu.VMEM((count, 2, SPAN, HD), jnp.bfloat16), pltpu.SemaphoreType.DMA((len(sources),))]
    if last:
        scratch += [pltpu.VMEM(*kind) for kind in STATE]
    if with_own:
        scratch.append(pltpu.VMEM((2, 2, SPAN, HD), jnp.bfloat16))
    dense = [query, *state] + ([spread] if with_own else [])
    pairs = 2 * SPAN * FT * (CF * count + 2 * with_own) * 3 // 4
    return pl.pallas_call(
        functools.partial(attend_kernel, first_piece, layout, with_own, last),
        out_shape=outs,
        in_specs=[SMEM] + [VMEM] * len(dense) + [ANY] * len(sources),
        out_specs=[VMEM] * len(outs),
        scratch_shapes=scratch,
        compiler_params=pltpu.CompilerParams(vmem_limit_bytes=VMEM_LIMIT),
        cost_estimate=pl.CostEstimate(flops=8 * pairs * HD, bytes_accessed=8 << 20, transcendentals=pairs),
        name=name,
    )(info, *dense, *sources)


def split_kernel(window_ref, cache_ref, mine_ref, other_ref):
    odd = lax.axis_index("yl") == 1
    low, high = cache_ref[..., :HD], cache_ref[..., HD:]
    mine_ref[...] = jnp.where(odd, high, low)
    other_ref[:, pl.ds(0, cache_ref.shape[1]), :] = jnp.where(odd, low, high)
    note = other_ref.at[:, pl.ds(cache_ref.shape[1], NOTE), :]
    note[...] = jnp.full(note.shape, window_ref[0], jnp.int32).astype(other_ref.dtype)


def split(window, cache):
    kinds, length, both = cache.shape
    return pl.pallas_call(
        split_kernel,
        grid=(kinds,),
        out_shape=(
            jax.ShapeDtypeStruct((kinds, length, both // 2), cache.dtype),
            jax.ShapeDtypeStruct((kinds, length + NOTE, both // 2), cache.dtype),
        ),
        in_specs=[SMEM, pl.BlockSpec((1, length, both), lambda i: (i, 0, 0))],
        out_specs=(
            pl.BlockSpec((1, length, both // 2), lambda i: (i, 0, 0)),
            pl.BlockSpec((1, length + NOTE, both // 2), lambda i: (i, 0, 0)),
        ),
        compiler_params=pltpu.CompilerParams(vmem_limit_bytes=VMEM_LIMIT),
        name="split",
    )(window, cache)


def lay_out_kernel(tokens_ref, after_ref, query_ref, own_ref):
    for j in range(query_ref.shape[1]):
        for side in range(2):
            columns = pl.ds((2 * j + side) * HD, HD)
            query_ref[side, j] = tokens_ref[0, :, columns]
            own_ref[side, j, 0] = tokens_ref[1, :, columns]
            own_ref[side, j, 1] = tokens_ref[2, :, columns]


def lay_out(tokens, after, steps=2):
    parts, rows, width = tokens.shape
    pairs = width // (2 * HD)
    step = pairs // steps
    return pl.pallas_call(
        lay_out_kernel,
        grid=(steps,),
        out_shape=(
            jax.ShapeDtypeStruct((2, pairs, rows, HD), tokens.dtype),
            jax.ShapeDtypeStruct((2, pairs, 2, rows, HD), tokens.dtype),
        ),
        in_specs=[pl.BlockSpec((parts, rows, 2 * step * HD), lambda i: (0, 0, i)), ANY],
        out_specs=(
            pl.BlockSpec((2, step, rows, HD), lambda i: (0, i, 0, 0)),
            pl.BlockSpec((2, step, 2, rows, HD), lambda i: (0, i, 0, 0, 0)),
        ),
        compiler_params=pltpu.CompilerParams(vmem_limit_bytes=VMEM_LIMIT),
        name="lay_out",
    )(tokens, after)


def by_token_kernel(heads_ref, out_ref):
    sides, pairs, _, _ = heads_ref.shape
    for side in range(sides):
        for j in range(pairs):
            out_ref[:, pl.ds((sides * j + side) * HD, HD)] = heads_ref[side, j]


def by_token(heads, steps=4):
    sides, pairs, rows, _ = heads.shape
    step = pairs // steps
    return pl.pallas_call(
        by_token_kernel,
        grid=(steps,),
        out_shape=jax.ShapeDtypeStruct((rows, sides * pairs * HD), heads.dtype),
        in_specs=[pl.BlockSpec((sides, step, rows, HD), lambda i: (0, i, 0, 0))],
        out_specs=pl.BlockSpec((rows, sides * step * HD), lambda i: (0, i)),
        compiler_params=pltpu.CompilerParams(vmem_limit_bytes=VMEM_LIMIT),
        name="by_token",
    )(heads)


def pick_kernel(mine_ref, down_ref, own_ref, out_ref, sem):
    odd = lax.axis_index("yl") == 1
    final = lax.axis_index("z") == lax.axis_size("z") - 1

    def fetch(source):
        copy = pltpu.make_async_copy(source, out_ref, sem)
        copy.start()
        copy.wait()

    @pl.when(odd)
    def _():
        fetch(mine_ref)

    @pl.when(jnp.logical_and(jnp.logical_not(odd), final))
    def _():
        fetch(own_ref.at[1])

    @pl.when(jnp.logical_not(jnp.logical_or(odd, final)))
    def _():
        fetch(down_ref)


def pick(mine, down, own):
    return pl.pallas_call(
        pick_kernel,
        out_shape=jax.ShapeDtypeStruct(mine.shape, mine.dtype),
        in_specs=[ANY] * 3,
        out_specs=VMEM,
        scratch_shapes=[pltpu.SemaphoreType.DMA],
        compiler_params=pltpu.CompilerParams(vmem_limit_bytes=VMEM_LIMIT),
        name="pick",
    )(mine, down, own)


def advance_kernel(rows, swap_ref, down_ref, own_ref, got_ref, out_ref, kept, sem):
    odd = lax.axis_index("yl") == 1
    final = lax.axis_index("z") == lax.axis_size("z") - 1
    low, high = pl.ds(0, HD), pl.ds(HD, HD)

    def fetch(source):
        copy = pltpu.make_async_copy(source.at[:, pl.ds(0, SPAN), :], kept, sem)
        copy.start()
        copy.wait()

    @pl.when(jnp.logical_not(odd))
    def _():
        fetch(swap_ref)
        out_ref[:, :, low] = kept[...]
        out_ref[:, :, high] = got_ref[...]

    @pl.when(jnp.logical_and(odd, jnp.logical_not(final)))
    def _():
        fetch(down_ref)
        out_ref[:, :, low] = got_ref[...]
        out_ref[:, :, high] = kept[...]

    @pl.when(jnp.logical_and(odd, final))
    def _():
        fetch(own_ref.at[1])
        for j in range(SPAN // rows):
            for kind in range(2):
                start = (2 * j + kind) * rows
                source = (start // SPAN, pl.ds(start % SPAN, rows))
                out_ref[kind, pl.ds(j * rows, rows), low] = got_ref[source]
                out_ref[kind, pl.ds(j * rows, rows), high] = kept[source]


def advance(swap, down, own, got, rows):
    return pl.pallas_call(
        functools.partial(advance_kernel, rows),
        out_shape=jax.ShapeDtypeStruct((2, SPAN, 2 * HD), swap.dtype),
        in_specs=[ANY] * 3 + [VMEM],
        out_specs=VMEM,
        scratch_shapes=[pltpu.VMEM((2, SPAN, HD), swap.dtype), pltpu.SemaphoreType.DMA],
        compiler_params=pltpu.CompilerParams(vmem_limit_bytes=VMEM_LIMIT),
        cost_estimate=pl.CostEstimate(flops=0, bytes_accessed=6 << 20, transcendentals=0),
        name="advance",
    )(swap, down, own, got)


def turn(value, axis, steps):
    count = lax.axis_size(axis)
    return lax.ppermute(value, axis, [(i, (i + steps) % count) for i in range(count)])


def per_device(qkv, cache, window):
    z, yl = lax.axis_index("z"), lax.axis_index("yl")
    planes = lax.axis_size("z")
    rows = qkv.shape[1]
    heads = qkv.shape[3] // HD
    near = cache.shape[1]

    mine, other = split(window, cache.reshape(2, near * FT, 2 * HD))
    query, own = lay_out(jnp.swapaxes(qkv[0], 0, 1), other)
    query = lax.all_to_all(query.reshape(heads, rows, HD), ("yl", "seq"), 0, 0, tiled=True).reshape(2, SPAN, HD)
    own = lax.all_to_all(own.reshape(heads, 2 * rows, HD), ("yl", "seq"), 0, 0, tiled=True)
    own = own.reshape(2, heads // 2, 2, rows, HD)
    swap = turn(other, "yl", 1)
    mine_up, mine_down = turn(mine, "z", 1), turn(mine, "z", -1)
    swap_up, swap_down = turn(swap, "z", 1), turn(swap, "z", -1)
    mine_far = [turn(mine_up[0], "z", 1), turn(mine_down[1], "z", -1)]
    swap_far = turn(swap, "z", 2)

    window_other = swap[0, near * FT, :1].astype(jnp.int32)
    windows = jnp.where(yl == 0, jnp.concatenate([window, window_other]), jnp.concatenate([window_other, window]))
    plane = jnp.array([0, -1, 1, 0, 2, -1, 1, 2], jnp.int32)
    side = jnp.where(jnp.array([0, 0, 0, 1, 0, 1, 1, 1]) == 0, yl, 1 - yl)
    bases = near * (2 * ((z + plane) % planes) + side)
    info = jnp.concatenate([windows, bases]).astype(jnp.int32)

    state = attend(info, query, (), None, [[mine], [mine_up], [mine_down], [swap], mine_far], 0, False, "attend_early")
    (result,) = attend(info, query, state, own, [[swap_up], [swap_down], [swap_far]], 5, True, "attend_late")
    returned = lax.all_to_all(result.reshape(heads, rows, HD), ("yl", "seq"), 0, 0, tiled=True)
    attended = by_token(returned.reshape(2, heads // 2, rows, HD))[None]

    own = own.reshape(2, 2, SPAN, HD)
    got = turn(pick(mine, mine_down, own), "yl", 1)
    return attended, advance(swap, swap_down, own, got, rows).reshape(cache.shape)


def solution(mesh):
    parts = Mesh(mesh.devices.reshape(4, 2, 16), ("z", "yl", "seq"))
    section = ("z", "yl")
    in_specs = (P(section, "seq", None, None), P(None, section, None, "seq"), P(section))
    out_specs = (P(section, "seq", None), P(None, section, None, "seq"))
    return jax.shard_map(
        per_device, mesh=parts, in_specs=in_specs, out_specs=out_specs, check_vma=False
    )
```

```python
import functools
import math

import jax
import jax.numpy as jnp
from jax import lax
from jax.experimental import pallas as pl
from jax.experimental.pallas import tpu as pltpu
from jax.sharding import Mesh, PartitionSpec as P

HD = 128
CF = 3
FT = 512
SPAN = 1536
CFR = 24
BASES = 2
NOTE = 16
SCALE = math.log2(math.e) / math.sqrt(HD)
TRUST = 2.0**100
VMEM_LIMIT = 46 << 20


def score(query, keys):
    scores = lax.dot_general(keys, query, (((1,), (1,)), ((), ())), preferred_element_type=jnp.float32)
    return scores * SCALE


def mix(weights, values):
    return lax.dot_general(
        values, weights.astype(jnp.bfloat16), (((0,), (0,)), ((), ())), preferred_element_type=jnp.float32
    )


def fold(weights):
    return jnp.sum(weights.reshape(weights.shape[0] // 8, 8, weights.shape[1]), axis=0)


def highest(scores):
    return jnp.broadcast_to(jnp.max(scores, axis=0, keepdims=True), (8, scores.shape[1]))


def tile_of(part):
    return pl.ds(pl.multiple_of(part * FT, FT), FT)


def attend_kernel(first_piece, layout, with_own, last, *refs):
    refs = list(refs)
    info_ref, query_ref = refs.pop(0), refs.pop(0)
    if first_piece:
        acc_in_ref, total_in_ref, top_in_ref = refs.pop(0), refs.pop(0), refs.pop(0)
    if with_own:
        spread_ref = refs.pop(0)
    sources = [refs.pop(0) for parts in layout for _ in parts]
    if last:
        out_ref = refs.pop(0)
    else:
        acc_ref, total_ref, top_ref = refs.pop(0), refs.pop(0), refs.pop(0)
    pieces, sems = refs.pop(0), refs.pop(0)
    if last:
        acc_ref, total_ref, top_ref = refs.pop(0), refs.pop(0), refs.pop(0)
    if with_own:
        own = refs.pop(0)

    count = len(layout)
    copies, at = [], 0
    for i, parts in enumerate(layout):
        copies.append([])
        for part in parts:
            target = pieces.at[i] if part is None else pieces.at[i, part]
            source = sources[at].at[..., pl.ds(0, SPAN), :]
            copies[-1].append(pltpu.make_async_copy(source, target, sems.at[at]))
            copies[-1][-1].start()
            at += 1

    def first_frame(section, piece):
        return jnp.clip(CFR - info_ref[section] - info_ref[BASES + first_piece + piece], 0, CF)

    def blank(section, piece):
        newest = lax.fori_loop(
            0, first_piece + piece, lambda i, most: jnp.maximum(most, info_ref[BASES + i]), jnp.int32(-CFR)
        )
        return newest + CF <= CFR - info_ref[section]

    def begin(section):
        if first_piece:
            acc_ref[section] = acc_in_ref[section]
            total_ref[section] = total_in_ref[section]
            top_ref[section] = top_in_ref[section]
        else:
            acc_ref[section] = jnp.zeros(acc_ref.shape[1:], acc_ref.dtype)
            total_ref[section] = jnp.zeros(total_ref.shape[1:], total_ref.dtype)
            top_ref[section] = jnp.zeros(top_ref.shape[1:], top_ref.dtype)

    begin(0)
    begin(1)

    def add(section, tile, keys, values):
        weights = jnp.exp2(score(query_ref[section, tile, :], keys) - top_ref[section, :1, tile])
        total_ref[section, :, tile] += fold(weights)
        acc_ref[section, :, tile] += mix(weights, values)

    if with_own:
        def add_own(section, carry):
            for j in range(spread_ref.shape[1]):
                rows = pl.ds(j * spread_ref.shape[3], spread_ref.shape[3])
                own[section, 0, rows, :] = spread_ref[section, j, 0]
                own[section, 1, rows, :] = spread_ref[section, j, 1]

            @pl.when(blank(section, 0))
            def _():
                for i in range(CF):
                    tile = pl.ds(i * FT, FT)
                    top_ref[section, :, tile] = highest(score(query_ref[section, tile, :], own[section, 0, tile, :]))

            for i in range(CF):
                keys = pl.ds(0, (i + 1) * FT)
                add(section, pl.ds(i * FT, FT), own[section, 0, keys, :], own[section, 1, keys, :])
            return carry

        lax.fori_loop(0, 2, add_own, 0)

    def one(index, carry):
        piece, section = index // 2, index % 2
        for i in range(count):
            @pl.when(index == 2 * i)
            def _():
                for copy in copies[i]:
                    copy.wait()

        first = first_frame(section, piece)
        everyone = pl.ds(0, SPAN)
        if not with_own:
            @pl.when(jnp.logical_and(first < CF, blank(section, piece)))
            def _():
                top_ref[section] = highest(score(query_ref[section], pieces[piece, 0, tile_of(first), :]))

        @pl.when(first == 0)
        def _():
            add(section, everyone, pieces[piece, 0], pieces[piece, 1])

        @pl.when(first > 0)
        def _():
            def frame(f, inner):
                add(section, everyone, pieces[piece, 0, tile_of(f), :], pieces[piece, 1, tile_of(f), :])
                return inner

            lax.fori_loop(first, CF, frame, 0)

        return carry

    lax.fori_loop(0, 2 * count, one, 0)

    def check(section, carry):
        safe = jnp.max(total_ref[section]) < TRUST

        @pl.when(jnp.logical_not(safe))
        def _():
            begin(section)

            @pl.when(blank(section, 0))
            def _():
                top_ref[section] = jnp.full(top_ref.shape[1:], -1e30, top_ref.dtype)

            def update(tile, keys, values):
                scores = score(query_ref[section, tile, :], keys)
                before = top_ref[section, :, tile]
                top = jnp.maximum(before, highest(scores))
                factor = jnp.exp2(before - top)
                weights = jnp.exp2(scores - top[:1])
                total_ref[section, :, tile] = total_ref[section, :, tile] * factor + fold(weights)
                acc_ref[section, :, tile] = acc_ref[section, :, tile] * factor[:1] + mix(weights, values)
                top_ref[section, :, tile] = top

            def again(part, inner):
                tile = tile_of(part)
                if with_own:
                    def own_frame(f, deep):
                        update(tile, own[section, 0, tile_of(f), :], own[section, 1, tile_of(f), :])
                        return deep

                    lax.fori_loop(0, part + 1, own_frame, 0)

                def one_piece(piece, deep):
                    def frame(f, deeper):
                        update(tile, pieces[piece, 0, tile_of(f), :], pieces[piece, 1, tile_of(f), :])
                        return deeper

                    lax.fori_loop(first_frame(section, piece), CF, frame, 0)
                    return deep

                lax.fori_loop(0, count, one_piece, 0)
                return inner

            lax.fori_loop(0, CF, again, 0)

        return carry

    lax.fori_loop(0, 2, check, 0)
    if last:
        def finish(section, carry):
            total = jnp.sum(total_ref[section], axis=0, keepdims=True)
            out_ref[section] = (acc_ref[section] / total).T.astype(jnp.bfloat16)
            return carry

        lax.fori_loop(0, 2, finish, 0)


SMEM = pl.BlockSpec(memory_space=pltpu.SMEM)
VMEM = pl.BlockSpec(memory_space=pltpu.VMEM)
ANY = pl.BlockSpec(memory_space=pl.ANY)
KV = ((2, SPAN, HD), jnp.bfloat16)
STATE = (((2, HD, SPAN), jnp.float32), ((2, 8, SPAN), jnp.float32), ((2, 8, SPAN), jnp.float32))


def attend(info, query, state, spread, groups, first_piece, last, name):
    layout = [(None,) if len(group) == 1 else (0, 1) for group in groups]
    sources = [array for group in groups for array in group]
    count, with_own = len(groups), spread is not None
    outs = [jax.ShapeDtypeStruct(*kind) for kind in ([KV] if last else STATE)]
    scratch = [pltpu.VMEM((count, 2, SPAN, HD), jnp.bfloat16), pltpu.SemaphoreType.DMA((len(sources),))]
    if last:
        scratch += [pltpu.VMEM(*kind) for kind in STATE]
    if with_own:
        scratch.append(pltpu.VMEM((2, 2, SPAN, HD), jnp.bfloat16))
    dense = [query, *state] + ([spread] if with_own else [])
    pairs = 2 * SPAN * FT * (CF * count + 2 * with_own) * 3 // 4
    return pl.pallas_call(
        functools.partial(attend_kernel, first_piece, layout, with_own, last),
        out_shape=outs,
        in_specs=[SMEM] + [VMEM] * len(dense) + [ANY] * len(sources),
        out_specs=[VMEM] * len(outs),
        scratch_shapes=scratch,
        compiler_params=pltpu.CompilerParams(vmem_limit_bytes=VMEM_LIMIT),
        cost_estimate=pl.CostEstimate(flops=8 * pairs * HD, bytes_accessed=8 << 20, transcendentals=pairs),
        name=name,
    )(info, *dense, *sources)


def split_kernel(window_ref, cache_ref, mine_ref, other_ref):
    odd = lax.axis_index("yl") == 1
    low, high = cache_ref[..., :HD], cache_ref[..., HD:]
    mine_ref[...] = jnp.where(odd, high, low)
    other_ref[:, pl.ds(0, cache_ref.shape[1]), :] = jnp.where(odd, low, high)
    note = other_ref.at[:, pl.ds(cache_ref.shape[1], NOTE), :]
    note[...] = jnp.full(note.shape, window_ref[0], jnp.int32).astype(other_ref.dtype)


def split(window, cache):
    kinds, length, both = cache.shape
    return pl.pallas_call(
        split_kernel,
        grid=(kinds,),
        out_shape=(
            jax.ShapeDtypeStruct((kinds, length, both // 2), cache.dtype),
            jax.ShapeDtypeStruct((kinds, length + NOTE, both // 2), cache.dtype),
        ),
        in_specs=[SMEM, pl.BlockSpec((1, length, both), lambda i: (i, 0, 0))],
        out_specs=(
            pl.BlockSpec((1, length, both // 2), lambda i: (i, 0, 0)),
            pl.BlockSpec((1, length + NOTE, both // 2), lambda i: (i, 0, 0)),
        ),
        compiler_params=pltpu.CompilerParams(vmem_limit_bytes=VMEM_LIMIT),
        name="split",
    )(window, cache)


def lay_out_kernel(tokens_ref, after_ref, query_ref, own_ref):
    for j in range(query_ref.shape[1]):
        for side in range(2):
            columns = pl.ds((2 * j + side) * HD, HD)
            query_ref[side, j] = tokens_ref[0, :, columns]
            own_ref[side, j, 0] = tokens_ref[1, :, columns]
            own_ref[side, j, 1] = tokens_ref[2, :, columns]


def lay_out(tokens, after, steps=2):
    parts, rows, width = tokens.shape
    pairs = width // (2 * HD)
    step = pairs // steps
    return pl.pallas_call(
        lay_out_kernel,
        grid=(steps,),
        out_shape=(
            jax.ShapeDtypeStruct((2, pairs, rows, HD), tokens.dtype),
            jax.ShapeDtypeStruct((2, pairs, 2, rows, HD), tokens.dtype),
        ),
        in_specs=[pl.BlockSpec((parts, rows, 2 * step * HD), lambda i: (0, 0, i)), ANY],
        out_specs=(
            pl.BlockSpec((2, step, rows, HD), lambda i: (0, i, 0, 0)),
            pl.BlockSpec((2, step, 2, rows, HD), lambda i: (0, i, 0, 0, 0)),
        ),
        compiler_params=pltpu.CompilerParams(vmem_limit_bytes=VMEM_LIMIT),
        name="lay_out",
    )(tokens, after)


def by_token_kernel(heads_ref, out_ref):
    sides, pairs, _, _ = heads_ref.shape
    for side in range(sides):
        for j in range(pairs):
            out_ref[:, pl.ds((sides * j + side) * HD, HD)] = heads_ref[side, j]


def by_token(heads, steps=4):
    sides, pairs, rows, _ = heads.shape
    step = pairs // steps
    return pl.pallas_call(
        by_token_kernel,
        grid=(steps,),
        out_shape=jax.ShapeDtypeStruct((rows, sides * pairs * HD), heads.dtype),
        in_specs=[pl.BlockSpec((sides, step, rows, HD), lambda i: (0, i, 0, 0))],
        out_specs=pl.BlockSpec((rows, sides * step * HD), lambda i: (0, i)),
        compiler_params=pltpu.CompilerParams(vmem_limit_bytes=VMEM_LIMIT),
        name="by_token",
    )(heads)


def pick_kernel(mine_ref, down_ref, own_ref, out_ref, sem):
    odd = lax.axis_index("yl") == 1
    final = lax.axis_index("z") == lax.axis_size("z") - 1

    def fetch(source):
        copy = pltpu.make_async_copy(source, out_ref, sem)
        copy.start()
        copy.wait()

    @pl.when(odd)
    def _():
        fetch(mine_ref)

    @pl.when(jnp.logical_and(jnp.logical_not(odd), final))
    def _():
        fetch(own_ref.at[1])

    @pl.when(jnp.logical_not(jnp.logical_or(odd, final)))
    def _():
        fetch(down_ref)


def pick(mine, down, own):
    return pl.pallas_call(
        pick_kernel,
        out_shape=jax.ShapeDtypeStruct(mine.shape, mine.dtype),
        in_specs=[ANY] * 3,
        out_specs=VMEM,
        scratch_shapes=[pltpu.SemaphoreType.DMA],
        compiler_params=pltpu.CompilerParams(vmem_limit_bytes=VMEM_LIMIT),
        name="pick",
    )(mine, down, own)


def advance_kernel(rows, swap_ref, down_ref, own_ref, got_ref, out_ref, kept, sem):
    odd = lax.axis_index("yl") == 1
    final = lax.axis_index("z") == lax.axis_size("z") - 1
    low, high = pl.ds(0, HD), pl.ds(HD, HD)

    def fetch(source):
        copy = pltpu.make_async_copy(source.at[:, pl.ds(0, SPAN), :], kept, sem)
        copy.start()
        copy.wait()

    @pl.when(jnp.logical_not(odd))
    def _():
        fetch(swap_ref)
        out_ref[:, :, low] = kept[...]
        out_ref[:, :, high] = got_ref[...]

    @pl.when(jnp.logical_and(odd, jnp.logical_not(final)))
    def _():
        fetch(down_ref)
        out_ref[:, :, low] = got_ref[...]
        out_ref[:, :, high] = kept[...]

    @pl.when(jnp.logical_and(odd, final))
    def _():
        fetch(own_ref.at[1])
        for j in range(SPAN // rows):
            for kind in range(2):
                start = (2 * j + kind) * rows
                source = (start // SPAN, pl.ds(start % SPAN, rows))
                out_ref[kind, pl.ds(j * rows, rows), low] = got_ref[source]
                out_ref[kind, pl.ds(j * rows, rows), high] = kept[source]


def advance(swap, down, own, got, rows):
    return pl.pallas_call(
        functools.partial(advance_kernel, rows),
        out_shape=jax.ShapeDtypeStruct((2, SPAN, 2 * HD), swap.dtype),
        in_specs=[ANY] * 3 + [VMEM],
        out_specs=VMEM,
        scratch_shapes=[pltpu.VMEM((2, SPAN, HD), swap.dtype), pltpu.SemaphoreType.DMA],
        compiler_params=pltpu.CompilerParams(vmem_limit_bytes=VMEM_LIMIT),
        cost_estimate=pl.CostEstimate(flops=0, bytes_accessed=6 << 20, transcendentals=0),
        name="advance",
    )(swap, down, own, got)


def turn(value, axis, steps):
    count = lax.axis_size(axis)
    return lax.ppermute(value, axis, [(i, (i + steps) % count) for i in range(count)])


def per_device(qkv, cache, window):
    z, yl = lax.axis_index("z"), lax.axis_index("yl")
    planes = lax.axis_size("z")
    rows = qkv.shape[1]
    heads = qkv.shape[3] // HD
    near = cache.shape[1]

    mine, other = split(window, cache.reshape(2, near * FT, 2 * HD))
    query, own = lay_out(jnp.swapaxes(qkv[0], 0, 1), other)
    query = lax.all_to_all(query.reshape(heads, rows, HD), ("yl", "seq"), 0, 0, tiled=True).reshape(2, SPAN, HD)
    own = lax.all_to_all(own.reshape(heads, 2 * rows, HD), ("yl", "seq"), 0, 0, tiled=True)
    own = own.reshape(2, heads // 2, 2, rows, HD)
    swap = turn(other, "yl", 1)
    mine_up, mine_down = turn(mine, "z", 1), turn(mine, "z", -1)
    swap_up, swap_down = turn(swap, "z", 1), turn(swap, "z", -1)
    mine_far = [turn(mine_up[0], "z", 1), turn(mine_down[1], "z", -1)]
    swap_far = turn(swap, "z", 2)

    window_other = swap[0, near * FT, :1].astype(jnp.int32)
    windows = jnp.where(yl == 0, jnp.concatenate([window, window_other]), jnp.concatenate([window_other, window]))
    plane = jnp.array([0, -1, 1, 0, 2, -1, 1, 2], jnp.int32)
    side = jnp.where(jnp.array([0, 0, 0, 1, 0, 1, 1, 1]) == 0, yl, 1 - yl)
    bases = near * (2 * ((z + plane) % planes) + side)
    info = jnp.concatenate([windows, bases]).astype(jnp.int32)

    state = attend(info, query, (), None, [[mine], [mine_up], [mine_down], [swap], mine_far], 0, False, "attend_early")
    (result,) = attend(info, query, state, own, [[swap_up], [swap_down], [swap_far]], 5, True, "attend_late")
    returned = lax.all_to_all(result.reshape(heads, rows, HD), ("yl", "seq"), 0, 0, tiled=True)
    attended = by_token(returned.reshape(2, heads // 2, rows, HD))[None]

    own = own.reshape(2, 2, SPAN, HD)
    got = turn(pick(mine, mine_down, own), "yl", 1)
    return attended, advance(swap, swap_down, own, got, rows).reshape(cache.shape)


def solution(mesh):
    parts = Mesh(mesh.devices.reshape(4, 2, 16), ("z", "yl", "seq"))
    section = ("z", "yl")
    in_specs = (P(section, "seq", None, None), P(None, section, None, "seq"), P(section))
    out_specs = (P(section, "seq", None), P(None, section, None, "seq"))
    return jax.shard_map(
        per_device, mesh=parts, in_specs=in_specs, out_specs=out_specs, check_vma=False
    )
```
